512 devices in a mesh: dp: 8 (over x, core), centers: 64 (over z, y).
Axes of the slice: x: 4, y: 8, z: 8, core: 2. Of those that a mesh axis runs over, the one named last changes fastest.
Arguments:
- features: bfloat16 [64, 32768], P(None, 'dp'), may hold values from -8 to 8
- prices: float32 [32768], P('dp'), may hold values from -6 to 6
- slots: int32 [32768], P('dp'), may hold values from 0 to 7
- center_idx: int32 [32768], P('centers'), may hold values from 0 to 32767
- center_scale: float32 [32768], P('centers'), may hold values from 0.5 to 18
Outputs:
- coefficients: float32 [8, 32768], P(None, 'centers')
- residual: float32 [8, 32768], P(None, 'centers')
The draws below stay inside these ranges and needn't reach their ends.
All inputs are finite; a program needn't handle non-finite values.
Results may differ from the reference program's by a relative error of at most 0.00195.
Values may be sent and summed in bfloat16 or wider, within the bound.
A program may use at most 64 MiB of HBM per device.

```python
import math
import jax
import jax.numpy as jnp
from jax import lax

F = 64
SLOTS = 8
ITERS = 2
NN = 32768
M = 32768


cluster_count = 256


def draw_features(key, part):
    key = jax.random.fold_in(key, 5)
    mean_key, member_key, noise_key = jax.random.split(key, 3)
    member = jax.random.randint(member_key, (NN,), 0, cluster_count)
    centres = 1.2 * jax.random.normal(mean_key, (F, cluster_count), jnp.float32)
    noise = jax.random.normal(noise_key, (F, NN), jnp.float32)
    return jnp.clip(jnp.take(centres, member, axis=1) + noise, -8.0, 8.0).astype(jnp.bfloat16)


def draw_center_scale(key, part):
    key = jax.random.fold_in(key, 11)
    position = jnp.arange(M, dtype=jnp.float32) / jnp.float32(max(M - 1, 1))
    factor = jnp.exp(jax.random.uniform(key, (M,), jnp.float32, -0.69, 0.69))
    return 3.0 ** position * factor


def place_ends(array, own_key, smallest, high):
    spot = [jax.random.randint(jax.random.fold_in(own_key, axis), (), 0, length) for axis, length in enumerate(array.shape)]
    widest = array.shape.index(max(array.shape))
    beside = spot[:widest] + [(spot[widest] + 1) % array.shape[widest]] + spot[widest + 1:]
    return array.at[tuple(spot)].set(smallest).at[tuple(beside)].set(high)


def level_of(own_key, shape, cuts, low, top_value):
    level, own = 1.0, jax.random.fold_in(own_key, 6)
    for dim, parts in cuts:
        draws = jnp.exp(jax.random.uniform(jax.random.fold_in(own, dim), (parts,), jnp.float32, low / len(cuts), top_value / len(cuts)))
        level = level * jnp.repeat(draws, shape[dim] // parts).reshape([-1 if axis == dim else 1 for axis in range(len(shape))])
    return level


def gaussian(rng, extent, spread, most, pieces=(), kind=jnp.bfloat16):
    drawn = spread * jax.random.normal(rng, extent, jnp.float32)
    if pieces:
        drawn = drawn * level_of(rng, extent, pieces, -0.22, 0.18)
    return jnp.clip(drawn, -most, most).astype(kind)


def setup_inputs(seed: int = 0) -> dict:
    streams_of = jax.random.split(jax.random.key(seed), 6)
    return {
        "features": draw_features(jax.random.fold_in(streams_of[5], 71), 0),
        "prices": gaussian(streams_of[1], (NN,), 1.0, 6.0, ((0, 8),), jnp.float32),
        "slots": place_ends(jax.random.randint(streams_of[2], (NN,), 0, SLOTS), jax.random.fold_in(streams_of[2], 1), 0, SLOTS - 1).astype(jnp.int32),
        "center_idx": place_ends(jax.random.randint(streams_of[3], (M,), 0, NN), jax.random.fold_in(streams_of[3], 1), 0, NN - 1).astype(jnp.int32),
        "center_scale": draw_center_scale(jax.random.fold_in(streams_of[5], 71), 0),
    }


highest_prec = lax.Precision.HIGHEST
ridge_shift = 0.5

def kernel_block(columns, center_f, center_norm):
    inner_prod = jnp.dot(columns.T, center_f, precision=highest_prec)
    row_norm = lax.optimization_barrier(jnp.sum(columns * columns, axis=0))
    return jnp.exp(-(row_norm[:, None] + center_norm[None, :] - 2.0 * inner_prod) / (2.0 * F))

def reference(features, prices, slots, center_idx, center_scale):
    feat32 = features.astype(jnp.float32)
    center_f = jnp.take(feat32, center_idx.astype(jnp.int32), axis=1)
    center_norm = lax.optimization_barrier(jnp.sum(center_f * center_f, axis=0))
    slot_mask = (slots[:, None] == jnp.arange(SLOTS, dtype=jnp.int32)[None, :]).astype(jnp.float32)
    block_len = math.gcd(NN, 1024)
    blocks = NN // block_len
    feat_blocks = jnp.transpose(feat32.reshape(F, blocks, block_len), (1, 0, 2))
    mask_blocks = slot_mask.reshape(blocks, block_len, SLOTS)
    price_blocks = prices.reshape(blocks, block_len)

    def full_pass(scaled, use_prices):

        def visit(summed, items):
            columns, masks, block_price = items
            kernel_tile = kernel_block(columns, center_f, center_norm)
            if use_prices:
                weights = masks * block_price[:, None]
            else:
                weights = masks * jnp.dot(kernel_tile, scaled.T, precision=highest_prec)
            return (summed + jnp.dot(weights.T, kernel_tile, precision=highest_prec), None)
        start_sum = jnp.zeros((SLOTS, M), jnp.float32)
        summed, unused = lax.scan(visit, start_sum, (feat_blocks, mask_blocks, price_blocks))
        return summed
    target_side = center_scale[None, :] * full_pass(jnp.zeros((SLOTS, M), jnp.float32), True) / jnp.sqrt(jnp.float32(NN))

    def hessian_apply(vector):
        summed = full_pass(center_scale[None, :] * vector, False)
        return center_scale[None, :] * summed / jnp.float32(NN) + ridge_shift * vector
    coefficients = jnp.zeros((SLOTS, M), jnp.float32)
    residual = target_side
    direction = target_side
    norm_now = lax.optimization_barrier(jnp.sum(residual * residual, axis=1))
    for iteration in range(ITERS):
        applied = hessian_apply(direction)
        step_size = norm_now / lax.optimization_barrier(jnp.sum(direction * applied, axis=1))
        coefficients = coefficients + step_size[:, None] * direction
        residual = residual - step_size[:, None] * applied
        norm_next = lax.optimization_barrier(jnp.sum(residual * residual, axis=1))
        direction = residual + (norm_next / norm_now)[:, None] * direction
        norm_now = norm_next
    return (coefficients, residual)
```

```python
import functools
import math

import jax
import jax.numpy as jnp
from jax import lax
from jax.experimental import pallas as pl
from jax.experimental.pallas import tpu as pltpu
from jax.sharding import PartitionSpec as P

SLOTS = 8
RIDGE = 0.5
MESH = pl.DeviceIdType.MESH
BF = jnp.bfloat16
F32 = jnp.float32

CHIPS_X = 4
RING = 8
LANE = 128


def dot_nn(a, b):
    return lax.dot_general(a, b, (((1,), (0,)), ((), ())), preferred_element_type=F32)


def dot_nt(a, b):
    return lax.dot_general(a, b, (((1,), (1,)), ((), ())), preferred_element_type=F32)


def split_rows(value):
    high = value.astype(BF).astype(F32)
    rest = value - high
    middle = rest.astype(BF).astype(F32)
    return jnp.concatenate([high, middle, rest - middle], axis=0).astype(BF)


def split_sum(rows24):
    return rows24[:SLOTS] + (rows24[SLOTS : 2 * SLOTS] + rows24[2 * SLOTS :])


def column_to_row(column):
    lane = lax.broadcasted_iota(jnp.int32, (SLOTS, LANE), 1)
    sub = lax.broadcasted_iota(jnp.int32, (SLOTS, LANE), 0)
    return jnp.sum(jnp.where(lane == sub, column, 0.0), axis=0, keepdims=True)


def row_to_column(row):
    lane = lax.broadcasted_iota(jnp.int32, (SLOTS, LANE), 1)
    sub = lax.broadcasted_iota(jnp.int32, (SLOTS, LANE), 0)
    return jnp.sum(jnp.where(lane == sub, row, 0.0), axis=1, keepdims=True)


def lane_blocks(value):
    return sum(value[:, j : j + LANE] for j in range(0, value.shape[1], LANE))


def kernel(
    total_rows,
    feat, price, slots, idx, scale,
    coef_out, resid_out,
    feat_t, e_hi, e_lo, cent, a_row, g_row,
    buf_ac, buf_ax, buf_yx, buf_yc, buf_p1, buf_p2,
    send_sem, recv_sem,
):
    f_dim, rows = feat.shape
    cols = idx.shape[1]
    half_c = cols // 2
    half_n = rows // 2
    tile = 256

    dp = lax.axis_index("dp")
    cen = lax.axis_index("centers")
    x_me, core_me = dp // 2, lax.rem(dp, 2)
    z_me, y_me = cen // RING, lax.rem(cen, RING)
    mate = [(dp + 1 - 2 * core_me, cen)]
    x_peers = [(lax.rem(dp + 2 * k, 2 * CHIPS_X), cen) for k in range(1, CHIPS_X)]
    y_peers = [(dp, z_me * RING + lax.rem(y_me + k, RING)) for k in range(1, RING)]
    z_peers = [(dp, lax.rem(z_me + k, RING) * RING + y_me) for k in range(1, RING)]

    barrier = pltpu.get_barrier_semaphore()
    everyone = mate + x_peers + y_peers + z_peers
    for peer in everyone:
        pl.semaphore_signal(barrier, inc=1, device_id=peer, device_id_type=MESH)

    used = [0]

    def start(ref, peers):
        copies = []
        for peer in peers:
            j = used[0]
            used[0] += 1
            copy = pltpu.make_async_remote_copy(
                src_ref=ref, dst_ref=ref, send_sem=send_sem.at[j], recv_sem=recv_sem.at[j],
                device_id=peer, device_id_type=MESH,
            )
            copy.start()
            copies.append(copy)
        return copies

    def finish(copies):
        for copy in copies:
            copy.wait_send()
        for copy in copies:
            copy.wait_recv()

    local_idx = idx[...] - dp * rows
    picked = [jnp.zeros((f_dim, half_c), F32) for _ in range(2)]
    for t in range(0, rows, tile):
        row = lax.broadcasted_iota(jnp.int32, (tile, half_c), 0) + t
        block = feat[:, t : t + tile]
        for h in range(2):
            hot = jnp.where(row == local_idx[:, h * half_c : (h + 1) * half_c], 1.0, 0.0)
            picked[h] = picked[h] + dot_nn(block, hot.astype(BF))
    for h in range(2):
        buf_ac[h, core_me] = picked[h].astype(BF)

    slot_id = lax.broadcasted_iota(jnp.int32, (SLOTS, rows), 0)
    norm = jnp.zeros((1, rows), F32)
    for t in range(0, f_dim, 16):
        piece = feat[t : t + 16, :].astype(F32)
        norm = norm + jnp.sum(piece * piece, axis=0, keepdims=True)
    a_row[...] = jnp.exp(norm * (-1.0 / (2.0 * f_dim)))
    for t in range(0, rows, tile):
        feat_t[t : t + tile, :] = feat[:, t : t + tile].T

    pl.semaphore_wait(barrier, len(everyone))

    copies = [start(buf_ac.at[h, core_me], mate) for h in range(2)]
    later = []
    for h in range(2):
        finish(copies[h])
        buf_ax[h, x_me] = buf_ac[h, 0] + buf_ac[h, 1]
        later.append(start(buf_ax.at[h, x_me], x_peers))

    def spread(weights):
        return split_rows(jnp.where(slots[...] == slot_id, weights, 0.0))

    weights24 = spread(a_row[...] * price[...])
    factor = math.log2(math.e) / f_dim
    center_norm = []
    for h in range(2):
        finish(later[h])
        part = (buf_ax[h, 0] + buf_ax[h, 1]) + (buf_ax[h, 2] + buf_ax[h, 3])
        cent[...] = part
        part32 = part.astype(F32)
        center_norm.append(jnp.sum(part32 * part32, axis=0, keepdims=True))
        for t in range(0, rows, tile):
            inner = dot_nn(feat_t[t : t + tile, :], cent[...])
            value = jnp.exp2(inner * factor)
            high = value.astype(BF)
            e_hi[t : t + tile, h * half_c : (h + 1) * half_c] = high
            e_lo[t : t + tile, h * half_c : (h + 1) * half_c] = (value - high.astype(F32)).astype(BF)

    def fold(v24):
        return split_sum(dot_nn(v24, e_hi[...]) + dot_nn(v24, e_lo[...]))

    def over_dp(i, payload):
        buf_yx[i, x_me] = payload
        finish(start(buf_yx.at[i, x_me], x_peers))
        buf_yc[i, core_me] = (buf_yx[i, 0] + buf_yx[i, 1]) + (buf_yx[i, 2] + buf_yx[i, 3])
        finish(start(buf_yc.at[i, core_me], mate))
        return buf_yc[i, 0] + buf_yc[i, 1]

    def over_centers(i, vector, extras):
        w24 = split_rows(factor_c * vector)
        first = []
        for h in range(2):
            span = slice(h * half_n, (h + 1) * half_n)
            part = split_sum(dot_nt(w24, e_hi[span, :]) + dot_nt(w24, e_lo[span, :]))
            mask = slots[:, h * half_n : (h + 1) * half_n] == slot_id[:, :half_n]
            chosen = jnp.sum(jnp.where(mask, part, 0.0), axis=0, keepdims=True)
            place = y_me if h == 0 else z_me
            buf_p1[i, h, place, :, :half_n] = chosen
            buf_p1[i, h, place, :, half_n:] = column_to_row(extras[h])
            first.append(start(buf_p1.at[i, h, place], y_peers if h == 0 else z_peers))
        second = []
        for h in range(2):
            finish(first[h])
            place = z_me if h == 0 else y_me
            buf_p2[i, h, place] = sum_of(buf_p1, i, h)
            second.append(start(buf_p2.at[i, h, place], z_peers if h == 0 else y_peers))
        sums = []
        for h in range(2):
            finish(second[h])
            sums.append(sum_of(buf_p2, i, h))
        row = jnp.concatenate([sums[0][:, :half_n], sums[1][:, :half_n]], axis=1)
        return row, row_to_column(sums[0][:, half_n:]), row_to_column(sums[1][:, half_n:])

    def sum_of(buf, i, h):
        v = [buf[i, h, k] for k in range(RING)]
        return ((v[0] + v[1]) + (v[2] + v[3])) + ((v[4] + v[5]) + (v[6] + v[7]))

    def slot_sums(row):
        return lane_blocks(jnp.where(slots[...] == slot_id, row * row, 0.0))

    none = jnp.zeros((SLOTS, LANE), F32)
    target = over_dp(0, jnp.concatenate([fold(weights24), none], axis=1))[:, :cols]
    factor_c = scale[...] * jnp.exp(
        jnp.concatenate(center_norm, axis=1) * (-1.0 / (2.0 * f_dim))
    )
    target = factor_c * target * (1.0 / math.sqrt(total_rows))

    rr_part = jnp.sum(target * target, axis=1, keepdims=True)
    row, rr0, _ = over_centers(0, target, (rr_part, rr_part))
    g_row[...] = a_row[...] * row
    row = g_row[...]
    both = over_dp(
        1, jnp.concatenate([fold(spread(a_row[...] * row)), slot_sums(row)], axis=1)
    )
    curve = jnp.sum(both[:, cols:], axis=1, keepdims=True) * (1.0 / total_rows) + RIDGE * rr0
    applied = factor_c * both[:, :cols] * (1.0 / total_rows) + RIDGE * target
    step0 = rr0 / curve
    residual = target - step0 * applied

    rr_part = jnp.sum(residual * residual, axis=1, keepdims=True)
    rd_part = jnp.sum(residual * target, axis=1, keepdims=True)
    row, rr1, rd1 = over_centers(1, residual, (rr_part, rd_part))
    beta = rr1 / rr0
    beta_row = jnp.sum(jnp.where(slots[...] == slot_id, beta, 0.0), axis=0, keepdims=True)
    row = a_row[...] * row + beta_row * g_row[...]
    direction = residual + beta * target
    dd = rr1 + 2.0 * beta * rd1 + beta * beta * rr0
    both = over_dp(
        2, jnp.concatenate([fold(spread(a_row[...] * row)), slot_sums(row)], axis=1)
    )
    curve = jnp.sum(both[:, cols:], axis=1, keepdims=True) * (1.0 / total_rows) + RIDGE * dd
    applied = factor_c * both[:, :cols] * (1.0 / total_rows) + RIDGE * direction
    step1 = rr1 / curve
    coef_out[...] = step0 * target + step1 * direction
    resid_out[...] = residual - step1 * applied


def per_device(total_rows, features, prices, slots, center_idx, center_scale):
    f_dim, rows = features.shape
    cols = center_idx.shape[0]
    half_c, half_n = cols // 2, rows // 2
    copies = 2 * (1 + CHIPS_X - 1) + 3 * CHIPS_X + 2 * 4 * (RING - 1)
    vmem = pl.BlockSpec(memory_space=pltpu.VMEM)
    return pl.pallas_call(
        functools.partial(kernel, total_rows),
        out_shape=[jax.ShapeDtypeStruct((SLOTS, cols), F32)] * 2,
        in_specs=[vmem] * 5,
        out_specs=[vmem] * 2,
        scratch_shapes=[
            pltpu.VMEM((rows, f_dim), BF),
            pltpu.VMEM((rows, cols), BF),
            pltpu.VMEM((rows, cols), BF),
            pltpu.VMEM((f_dim, half_c), BF),
            pltpu.VMEM((1, rows), F32),
            pltpu.VMEM((1, rows), F32),
            pltpu.VMEM((2, 2, f_dim, half_c), BF),
            pltpu.VMEM((2, CHIPS_X, f_dim, half_c), BF),
            pltpu.VMEM((3, CHIPS_X, SLOTS, cols + LANE), F32),
            pltpu.VMEM((3, 2, SLOTS, cols + LANE), F32),
            pltpu.VMEM((2, 2, RING, 1, half_n + LANE), F32),
            pltpu.VMEM((2, 2, RING, 1, half_n + LANE), F32),
            pltpu.SemaphoreType.DMA((copies,)),
            pltpu.SemaphoreType.DMA((copies,)),
        ],
        compiler_params=pltpu.CompilerParams(
            collective_id=0, has_side_effects=True, vmem_limit_bytes=40 << 20
        ),
        name="cg_steps",
    )(
        features,
        prices.reshape(1, rows),
        slots.reshape(1, rows),
        center_idx.reshape(1, cols),
        center_scale.reshape(1, cols),
    )


def solution(mesh):
    def run(features, prices, slots, center_idx, center_scale):
        body = functools.partial(per_device, features.shape[1])
        return jax.shard_map(
            body,
            mesh=mesh,
            in_specs=(P(None, "dp"), P("dp"), P("dp"), P("centers"), P("centers")),
            out_specs=(P(None, "centers"), P(None, "centers")),
            check_vma=False,
        )(features, prices, slots, center_idx, center_scale)

    return run
```

```python
import functools
import math

import jax
import jax.numpy as jnp
from jax import lax
from jax.experimental import pallas as pl
from jax.experimental.pallas import tpu as pltpu
from jax.sharding import PartitionSpec as P

SLOTS = 8
RIDGE = 0.5
MESH = pl.DeviceIdType.MESH
BF = jnp.bfloat16
F32 = jnp.float32

RING = 8
PARTS = 4
LANE = 128


def dot_nn(a, b):
    return lax.dot_general(a, b, (((1,), (0,)), ((), ())), preferred_element_type=F32)


def dot_nt(a, b):
    return lax.dot_general(a, b, (((1,), (1,)), ((), ())), preferred_element_type=F32)


def split_rows(value):
    high = value.astype(BF).astype(F32)
    rest = value - high
    middle = rest.astype(BF).astype(F32)
    return jnp.concatenate([high, middle, rest - middle], axis=0).astype(BF)


def split_sum(rows24):
    return rows24[:SLOTS] + (rows24[SLOTS : 2 * SLOTS] + rows24[2 * SLOTS : 3 * SLOTS])


def column_to_row(column):
    lane = lax.broadcasted_iota(jnp.int32, (SLOTS, LANE), 1)
    sub = lax.broadcasted_iota(jnp.int32, (SLOTS, LANE), 0)
    return jnp.sum(jnp.where(lane == sub, column, 0.0), axis=0, keepdims=True)


def row_to_column(row):
    lane = lax.broadcasted_iota(jnp.int32, (SLOTS, LANE), 1)
    sub = lax.broadcasted_iota(jnp.int32, (SLOTS, LANE), 0)
    return jnp.sum(jnp.where(lane == sub, row, 0.0), axis=1, keepdims=True)


def lane_blocks(value):
    return sum(value[:, j : j + LANE] for j in range(0, value.shape[1], LANE))


def kernel(
    total_rows,
    feat_in, price_in, slots_in, idx_in, scale_in,
    coef_out, resid_out,
    feat, price, slots, idx, scale,
    feat_t, e_hi, e_lo, t_hi, t_lo, a_row, g_row, weights,
    buf_a, buf_y0, buf_y1, buf_p1, buf_p2,
    load_sem, send_sem, recv_sem,
):
    f_dim, rows = feat.shape
    cols = idx.shape[1]
    half = cols // 2
    part_n = rows // PARTS
    tile = 256

    dp = lax.axis_index("dp")
    cen = lax.axis_index("centers")
    z_me, y_me = cen // RING, lax.rem(cen, RING)
    dp_peers = [(lax.rem(dp + k, RING), cen) for k in range(1, RING)]
    y_peers = [(dp, z_me * RING + lax.rem(y_me + k, RING)) for k in range(1, RING)]
    z_peers = [(dp, lax.rem(z_me + k, RING) * RING + y_me) for k in range(1, RING)]

    barrier = pltpu.get_barrier_semaphore()
    everyone = dp_peers + y_peers + z_peers
    loads = [
        pltpu.make_async_copy(src, dst, load_sem.at[j])
        for j, (src, dst) in enumerate(
            ((idx_in, idx), (feat_in, feat), (slots_in, slots), (price_in, price), (scale_in, scale))
        )
    ]
    for load in loads:
        load.start()
    for peer in everyone:
        pl.semaphore_signal(barrier, inc=1, device_id=peer, device_id_type=MESH)

    used = [0]

    def start(buf, me, peers):
        j = used[0]
        used[0] += 1
        for peer in peers:
            pltpu.make_async_remote_copy(
                src_ref=buf.at[me], dst_ref=buf.at[me], send_sem=send_sem.at[j], recv_sem=recv_sem.at[j],
                device_id=peer, device_id_type=MESH,
            ).start()
        return buf, j

    def finish(handle):
        buf, j = handle
        seven = buf.at[pl.ds(0, RING - 1)]
        pltpu.make_async_copy(seven, seven, send_sem.at[j]).wait()
        pltpu.make_async_copy(seven, seven, recv_sem.at[j]).wait()

    def total(buf):
        v = [buf[k] for k in range(RING)]
        return ((v[0] + v[1]) + (v[2] + v[3])) + ((v[4] + v[5]) + (v[6] + v[7]))

    loads[0].wait()
    loads[1].wait()
    local_idx = idx[...] - dp * rows
    for h in range(2):
        picked = jnp.zeros((f_dim, half), F32)
        for t in range(0, rows, tile):
            row = lax.broadcasted_iota(jnp.int32, (tile, half), 0) + t
            hot = jnp.where(row == local_idx[:, h * half : (h + 1) * half], 1.0, 0.0)
            picked = picked + dot_nn(feat[:, t : t + tile], hot.astype(BF))
        buf_a[h, dp] = picked.astype(BF)
    for load in loads[2:]:
        load.wait()
    pl.semaphore_wait(barrier, len(everyone))

    sent = [start(buf_a.at[h], dp, dp_peers) for h in range(2)]
    for t in range(0, rows, tile):
        feat_t[t : t + tile, :] = feat[:, t : t + tile].T
    norm = jnp.zeros((1, rows), F32)
    for t in range(0, f_dim, 16):
        piece = feat[t : t + 16, :].astype(F32)
        norm = norm + jnp.sum(piece * piece, axis=0, keepdims=True)
    a_row[...] = jnp.exp(norm * (-1.0 / (2.0 * f_dim)))

    def own_slot(n):
        span = slots[:, n]
        return span == lax.broadcasted_iota(jnp.int32, (SLOTS, span.shape[1]), 0)

    def columns(h):
        return slice(h * half, (h + 1) * half)

    def auctions(q):
        return slice(q * part_n, (q + 1) * part_n)

    for q in range(PARTS):
        n = auctions(q)
        v24 = split_rows(jnp.where(own_slot(n), a_row[:, n] * price[:, n], 0.0))
        weights[:, n] = jnp.concatenate([v24.astype(F32), jnp.zeros((SLOTS, part_n), F32)], axis=0).astype(BF)

    def fold(v24, n, h):
        m = columns(h)
        return dot_nn(v24, e_hi[n, m]) + dot_nn(v24, e_lo[n, m])

    factor = math.log2(math.e) / f_dim
    centers, center_norm, sums = [], [], []
    for h in range(2):
        finish(sent[h])
        part = total(buf_a.at[h])
        part32 = part.astype(F32)
        centers.append(part)
        center_norm.append(jnp.sum(part32 * part32, axis=0, keepdims=True))
        for t in range(0, rows, tile):
            value = jnp.exp2(dot_nn(feat_t[t : t + tile, :], part) * factor)
            high = value.astype(BF)
            e_hi[t : t + tile, columns(h)] = high
            e_lo[t : t + tile, columns(h)] = (value - high.astype(F32)).astype(BF)
        buf = (buf_y0 if h == 0 else buf_y1).at[0]
        buf[dp, :, :half] = split_sum(fold(weights[...], slice(0, rows), h))
        if h == 0:
            buf[dp, :, half:] = jnp.zeros((SLOTS, LANE), F32)
        sums.append(start(buf, dp, dp_peers))

    for h in range(2):
        turned = centers[h].T
        for t in range(0, rows, tile):
            value = jnp.exp2(dot_nn(turned, feat[:, t : t + tile]) * factor)
            high = value.astype(BF)
            t_hi[columns(h), t : t + tile] = high
            t_lo[columns(h), t : t + tile] = (value - high.astype(F32)).astype(BF)
    factor_c = [
        scale[:, columns(h)] * jnp.exp(center_norm[h] * (-1.0 / (2.0 * f_dim))) for h in range(2)
    ]

    def over_centers(i, vector, extras):
        w24 = split_rows(jnp.concatenate([factor_c[h] * vector[h] for h in range(2)], axis=1))
        rings = [(y_me, y_peers), (z_me, z_peers)]
        first = []
        for q in range(PARTS):
            n = auctions(q)
            part = split_sum(dot_nn(w24, t_hi[:, n]) + dot_nn(w24, t_lo[:, n]))
            place, peers = rings[q % 2]
            buf = buf_p1.at[i, q]
            buf[place, :, :part_n] = jnp.sum(
                jnp.where(own_slot(n), part, 0.0), axis=0, keepdims=True
            )
            buf[place, :, part_n:] = column_to_row(extras[min(q, 1)])
            first.append(start(buf, place, peers))
        second = []
        for q in range(PARTS):
            finish(first[q])
            place, peers = rings[1 - q % 2]
            buf = buf_p2.at[i, q]
            buf[place] = total(buf_p1.at[i, q])
            second.append(start(buf, place, peers))
        for q in range(PARTS):
            finish(second[q])
            yield total(buf_p2.at[i, q])

    def fold_over_dp(i, parts_of_g):
        acc = [jnp.zeros((3 * SLOTS, half), F32) for _ in range(2)]
        squares = jnp.zeros((SLOTS, LANE), F32)
        sums = []
        for q, row in enumerate(parts_of_g):
            n = auctions(q)
            mask = own_slot(n)
            squares = squares + lane_blocks(jnp.where(mask, row * row, 0.0))
            v24 = split_rows(jnp.where(mask, a_row[:, n] * row, 0.0))
            for h in range(2):
                acc[h] = acc[h] + fold(v24, n, h)
                if q == PARTS - 1:
                    buf = (buf_y0 if h == 0 else buf_y1).at[i]
                    buf[dp, :, :half] = split_sum(acc[h])
                    if h == 0:
                        buf[dp, :, half:] = squares
                    sums.append(start(buf, dp, dp_peers))
        return sums

    def arrived(i, sums):
        finish(sums[0])
        both = total(buf_y0.at[i])
        finish(sums[1])
        return [both[:, :half], total(buf_y1.at[i])], jnp.sum(both[:, half:], axis=1, keepdims=True)

    def dots(u, v):
        return sum(jnp.sum(u[h] * v[h], axis=1, keepdims=True) for h in range(2))

    folded, _ = arrived(0, sums)
    target = [factor_c[h] * folded[h] * (1.0 / math.sqrt(total_rows)) for h in range(2)]

    rr_part = dots(target, target)
    rr = []

    def first_sums():
        for q, row in enumerate(over_centers(0, target, (rr_part, rr_part))):
            if q == 0:
                rr.append(row_to_column(row[:, part_n:]))
            row = a_row[:, auctions(q)] * row[:, :part_n]
            g_row[:, auctions(q)] = row
            yield row

    folded, squares = arrived(1, fold_over_dp(1, first_sums()))
    step0 = rr[0] / (squares * (1.0 / total_rows) + RIDGE * rr[0])
    residual = []
    for h in range(2):
        applied = factor_c[h] * folded[h] * (1.0 / total_rows) + RIDGE * target[h]
        residual.append(target[h] - step0 * applied)

    rr_part, rd_part = dots(residual, residual), dots(residual, target)
    rd = []

    def second_sums():
        parts = over_centers(1, residual, (rr_part, rd_part))
        held = [next(parts), next(parts)]
        rr.append(row_to_column(held[0][:, part_n:]))
        rd.append(row_to_column(held[1][:, part_n:]))
        beta = rr[1] / rr[0]
        for q in range(PARTS):
            row = held[q] if q < 2 else next(parts)
            n = auctions(q)
            beta_row = jnp.sum(jnp.where(own_slot(n), beta, 0.0), axis=0, keepdims=True)
            yield a_row[:, n] * row[:, :part_n] + beta_row * g_row[:, n]

    sums = fold_over_dp(2, second_sums())
    beta = rr[1] / rr[0]
    direction = [residual[h] + beta * target[h] for h in range(2)]
    dd = rr[1] + 2.0 * beta * rd[0] + beta * beta * rr[0]
    folded, squares = arrived(2, sums)
    step1 = rr[1] / (squares * (1.0 / total_rows) + RIDGE * dd)
    for h in range(2):
        applied = factor_c[h] * folded[h] * (1.0 / total_rows) + RIDGE * direction[h]
        coef_out[:, columns(h)] = step0 * target[h] + step1 * direction[h]
        resid_out[:, columns(h)] = residual[h] - step1 * applied


def per_device(total_rows, features, prices, slots, center_idx, center_scale):
    f_dim, rows = features.shape
    cols = center_idx.shape[0]
    half, part_n = cols // 2, rows // PARTS
    exchanges = 2 + 3 * 2 + 2 * 2 * PARTS
    vmem = pl.BlockSpec(memory_space=pltpu.VMEM)
    return pl.pallas_call(
        functools.partial(kernel, total_rows),
        out_shape=[jax.ShapeDtypeStruct((SLOTS, cols), F32)] * 2,
        in_specs=[pl.BlockSpec(memory_space=pl.ANY)] * 5,
        out_specs=[vmem] * 2,
        scratch_shapes=[
            pltpu.VMEM((f_dim, rows), BF),
            pltpu.VMEM((1, rows), F32),
            pltpu.VMEM((1, rows), jnp.int32),
            pltpu.VMEM((1, cols), jnp.int32),
            pltpu.VMEM((1, cols), F32),
            pltpu.VMEM((rows, f_dim), BF),
            pltpu.VMEM((rows, cols), BF),
            pltpu.VMEM((rows, cols), BF),
            pltpu.VMEM((cols, rows), BF),
            pltpu.VMEM((cols, rows), BF),
            pltpu.VMEM((1, rows), F32),
            pltpu.VMEM((1, rows), F32),
            pltpu.VMEM((4 * SLOTS, rows), BF),
            pltpu.VMEM((2, RING, f_dim, half), BF),
            pltpu.VMEM((3, RING, SLOTS, half + LANE), F32),
            pltpu.VMEM((3, RING, SLOTS, half), F32),
            pltpu.VMEM((2, PARTS, RING, 1, part_n + LANE), F32),
            pltpu.VMEM((2, PARTS, RING, 1, part_n + LANE), F32),
            pltpu.SemaphoreType.DMA((5,)),
            pltpu.SemaphoreType.DMA((exchanges,)),
            pltpu.SemaphoreType.DMA((exchanges,)),
        ],
        compiler_params=pltpu.CompilerParams(
            collective_id=0, has_side_effects=True, vmem_limit_bytes=50 << 20
        ),
        name="cg_steps",
    )(
        features,
        prices.reshape(1, rows),
        slots.reshape(1, rows),
        center_idx.reshape(1, cols),
        center_scale.reshape(1, cols),
    )


def solution(mesh):
    def run(features, prices, slots, center_idx, center_scale):
        body = functools.partial(per_device, features.shape[1])
        return jax.shard_map(
            body,
            mesh=mesh,
            in_specs=(P(None, "dp"), P("dp"), P("dp"), P("centers"), P("centers")),
            out_specs=(P(None, "centers"), P(None, "centers")),
            check_vma=False,
        )(features, prices, slots, center_idx, center_scale)

    return run
```

```python
import functools
import math

import jax
import jax.numpy as jnp
from jax import lax
from jax.experimental import pallas as pl
from jax.experimental.pallas import tpu as pltpu
from jax.sharding import PartitionSpec as P

SLOTS = 8
RIDGE = 0.5
MESH = pl.DeviceIdType.MESH
BF = jnp.bfloat16
F32 = jnp.float32

RING = 8
CHIPS_X = 4
PARTS = 8
RR_PART, RD_PART = 1, 2
LANE = 128


def dot_nn(a, b):
    return lax.dot_general(a, b, (((1,), (0,)), ((), ())), preferred_element_type=F32)


def dot_nt(a, b):
    return lax.dot_general(a, b, (((1,), (1,)), ((), ())), preferred_element_type=F32)


def split_rows(value):
    high = value.astype(BF).astype(F32)
    rest = value - high
    middle = rest.astype(BF).astype(F32)
    return jnp.concatenate([high, middle, rest - middle], axis=0).astype(BF)


def split_sum(rows24):
    return rows24[:SLOTS] + (rows24[SLOTS : 2 * SLOTS] + rows24[2 * SLOTS : 3 * SLOTS])


def column_to_row(column):
    lane = lax.broadcasted_iota(jnp.int32, (SLOTS, LANE), 1)
    sub = lax.broadcasted_iota(jnp.int32, (SLOTS, LANE), 0)
    return jnp.sum(jnp.where(lane == sub, column, 0.0), axis=0, keepdims=True)


def row_to_column(row):
    lane = lax.broadcasted_iota(jnp.int32, (SLOTS, LANE), 1)
    sub = lax.broadcasted_iota(jnp.int32, (SLOTS, LANE), 0)
    return jnp.sum(jnp.where(lane == sub, row, 0.0), axis=1, keepdims=True)


def lane_blocks(value):
    return sum(value[:, j : j + LANE] for j in range(0, value.shape[1], LANE))


def kernel(
    total_rows,
    feat_in, price_in, slots_in, idx_in, scale_in,
    coef_out, resid_out,
    feat, price, slots, idx, scale,
    feat_t, e_hi, e_lo, t_hi, t_lo, a_row, g_row, weights, first_half,
    buf_ax, buf_ac, buf_y0, buf_y1, buf_p1, buf_p2,
    load_sem, send_sem, recv_sem,
):
    f_dim, rows = feat.shape
    cols = idx.shape[1]
    half = cols // 2
    part_n = rows // PARTS
    tile = 256

    dp = lax.axis_index("dp")
    cen = lax.axis_index("centers")
    z_me, y_me = cen // RING, lax.rem(cen, RING)
    x_me, core_me = dp // 2, lax.rem(dp, 2)
    dp_peers = [(lax.rem(dp + k, RING), cen) for k in range(1, RING)]
    x_peers = [(lax.rem(dp + 2 * k, RING), cen) for k in range(1, CHIPS_X)]
    mate = [(dp + 1 - 2 * core_me, cen)]
    y_peers = [(dp, z_me * RING + lax.rem(y_me + k, RING)) for k in range(1, RING)]
    z_peers = [(dp, lax.rem(z_me + k, RING) * RING + y_me) for k in range(1, RING)]

    barrier = pltpu.get_barrier_semaphore()
    everyone = dp_peers + y_peers + z_peers
    loads = [
        pltpu.make_async_copy(src, dst, load_sem.at[j])
        for j, (src, dst) in enumerate(
            ((idx_in, idx), (feat_in, feat), (slots_in, slots), (price_in, price), (scale_in, scale))
        )
    ]
    for load in loads:
        load.start()
    for peer in everyone:
        pl.semaphore_signal(barrier, inc=1, device_id=peer, device_id_type=MESH)

    used = [0]

    def start(buf, me, peers):
        j = used[0]
        used[0] += 1
        for peer in peers:
            pltpu.make_async_remote_copy(
                src_ref=buf.at[me], dst_ref=buf.at[me], send_sem=send_sem.at[j], recv_sem=recv_sem.at[j],
                device_id=peer, device_id_type=MESH,
            ).start()
        return buf.at[pl.ds(0, len(peers))], j

    def finish(handle):
        slots_of_peers, j = handle
        pltpu.make_async_copy(slots_of_peers, slots_of_peers, send_sem.at[j]).wait()
        pltpu.make_async_copy(slots_of_peers, slots_of_peers, recv_sem.at[j]).wait()

    def total(buf, count=RING):
        v = [buf[k] for k in range(count)]
        while len(v) > 1:
            v = [v[k] + v[k + 1] for k in range(0, len(v), 2)]
        return v[0]

    loads[0].wait()
    loads[1].wait()
    local_idx = idx[...] - dp * rows
    for h in range(2):
        picked = jnp.zeros((f_dim, half), F32)
        for t in range(0, rows, tile):
            row = lax.broadcasted_iota(jnp.int32, (tile, half), 0) + t
            hot = jnp.where(row == local_idx[:, h * half : (h + 1) * half], 1.0, 0.0)
            picked = picked + dot_nn(feat[:, t : t + tile], hot.astype(BF))
        buf_ax[h, x_me] = picked.astype(BF)
    for load in loads[2:]:
        load.wait()
    pl.semaphore_wait(barrier, len(everyone))

    sent = [start(buf_ax.at[h], x_me, x_peers) for h in range(2)]
    for t in range(0, rows, tile):
        feat_t[t : t + tile, :] = feat[:, t : t + tile].T
    norm = jnp.zeros((1, rows), F32)
    for t in range(0, f_dim, 16):
        piece = feat[t : t + 16, :].astype(F32)
        norm = norm + jnp.sum(piece * piece, axis=0, keepdims=True)
    a_row[...] = jnp.exp(norm * (-1.0 / (2.0 * f_dim)))

    def own_slot(n):
        span = slots[:, n]
        return span == lax.broadcasted_iota(jnp.int32, (SLOTS, span.shape[1]), 0)

    def columns(h):
        return slice(h * half, (h + 1) * half)

    def auctions(q):
        return slice(q * part_n, (q + 1) * part_n)

    for q in range(PARTS):
        n = auctions(q)
        v24 = split_rows(jnp.where(own_slot(n), a_row[:, n] * price[:, n], 0.0))
        weights[:, n] = jnp.concatenate([v24.astype(F32), jnp.zeros((SLOTS, part_n), F32)], axis=0).astype(BF)

    def fold(v24, n, h):
        m = columns(h)
        return dot_nn(v24, e_hi[n, m]) + dot_nn(v24, e_lo[n, m])

    factor = math.log2(math.e) / f_dim
    centers, center_norm, sums = [], [], []
    for h in range(2):
        finish(sent[h])
        buf_ac[h, core_me] = total(buf_ax.at[h], CHIPS_X)
        sent[h] = start(buf_ac.at[h], core_me, mate)
    for h in range(2):
        finish(sent[h])
        part = total(buf_ac.at[h], 2)
        part32 = part.astype(F32)
        centers.append(part)
        center_norm.append(jnp.sum(part32 * part32, axis=0, keepdims=True))
        for t in range(0, rows, tile):
            value = jnp.exp2(dot_nn(feat_t[t : t + tile, :], part) * factor)
            high = value.astype(BF)
            e_hi[t : t + tile, columns(h)] = high
            e_lo[t : t + tile, columns(h)] = (value - high.astype(F32)).astype(BF)
        buf = (buf_y0 if h == 0 else buf_y1).at[0]
        buf[dp, :, :half] = split_sum(fold(weights[...], slice(0, rows), h))
        if h == 0:
            buf[dp, :, half:] = jnp.zeros((SLOTS, LANE), F32)
        sums.append(start(buf, dp, dp_peers))

    for h in range(2):
        turned = centers[h].T
        for t in range(0, rows, tile):
            value = jnp.exp2(dot_nn(turned, feat[:, t : t + tile]) * factor)
            high = value.astype(BF)
            t_hi[columns(h), t : t + tile] = high
            t_lo[columns(h), t : t + tile] = (value - high.astype(F32)).astype(BF)
    factor_c = [
        scale[:, columns(h)] * jnp.exp(center_norm[h] * (-1.0 / (2.0 * f_dim))) for h in range(2)
    ]

    def apply_half(w, n, h):
        m = columns(h)
        return split_sum(dot_nn(w, t_hi[m, n]) + dot_nn(w, t_lo[m, n]))

    def over_centers(i, halves, column_of):
        w24 = split_rows(factor_c[0] * next(halves))
        for q in range(PARTS):
            n = auctions(q)
            first_half[:, n] = apply_half(w24, n, 0)
        w24 = split_rows(factor_c[1] * next(halves))
        rings = [(y_me, y_peers), (z_me, z_peers)]

        def of_part(buf, q):
            width = part_n + LANE if q in (RR_PART, RD_PART) else part_n
            return buf.at[i, q, :, :, pl.ds(0, width)]

        first = []
        for q in range(PARTS):
            n = auctions(q)
            part = first_half[:, n] + apply_half(w24, n, 1)
            place, peers = rings[q % 2]
            buf = of_part(buf_p1, q)
            chosen = jnp.sum(jnp.where(own_slot(n), part, 0.0), axis=0, keepdims=True)
            if q in (RR_PART, RD_PART):
                chosen = jnp.concatenate([chosen, column_to_row(column_of(q))], axis=1)
            buf[place] = chosen
            first.append(start(buf, place, peers))
        second = []
        for q in range(PARTS):
            finish(first[q])
            place, peers = rings[1 - q % 2]
            buf = of_part(buf_p2, q)
            buf[place] = total(of_part(buf_p1, q))
            second.append(start(buf, place, peers))
        for q in range(PARTS):
            finish(second[q])
            yield total(of_part(buf_p2, q))

    def fold_over_dp(i, parts_of_g):
        acc = [jnp.zeros((3 * SLOTS, half), F32) for _ in range(2)]
        squares = jnp.zeros((SLOTS, LANE), F32)
        sums = []
        for q, row in enumerate(parts_of_g):
            n = auctions(q)
            mask = own_slot(n)
            squares = squares + lane_blocks(jnp.where(mask, row * row, 0.0))
            v24 = split_rows(jnp.where(mask, a_row[:, n] * row, 0.0))
            for h in range(2):
                acc[h] = acc[h] + fold(v24, n, h)
                if q == PARTS - 1:
                    buf = (buf_y0 if h == 0 else buf_y1).at[i]
                    buf[dp, :, :half] = split_sum(acc[h])
                    if h == 0:
                        buf[dp, :, half:] = squares
                    sums.append(start(buf, dp, dp_peers))
        return sums

    def arrived(i, sums):
        finish(sums[0])
        both = total(buf_y0.at[i])
        yield both[:, :half], jnp.sum(both[:, half:], axis=1, keepdims=True)
        finish(sums[1])
        yield total(buf_y1.at[i]), None

    def dots(u, v):
        return sum(jnp.sum(u[h] * v[h], axis=1, keepdims=True) for h in range(2))

    target = []

    def target_halves():
        for h, (folded, _) in enumerate(arrived(0, sums)):
            target.append(factor_c[h] * folded * (1.0 / math.sqrt(total_rows)))
            yield target[h]

    rr = []

    def first_sums():
        parts = over_centers(0, target_halves(), lambda q: dots(target, target))
        for q, row in enumerate(parts):
            if q == RR_PART:
                rr.append(row_to_column(row[:, part_n:]))
            row = a_row[:, auctions(q)] * row[:, :part_n]
            g_row[:, auctions(q)] = row
            yield row

    sums_one = fold_over_dp(1, first_sums())

    residual, steps = [], []

    def residual_halves():
        for h, (folded, squares) in enumerate(arrived(1, sums_one)):
            if h == 0:
                steps.append(rr[0] / (squares * (1.0 / total_rows) + RIDGE * rr[0]))
            applied = factor_c[h] * folded * (1.0 / total_rows) + RIDGE * target[h]
            residual.append(target[h] - steps[0] * applied)
            yield residual[h]

    rd = []

    def second_sums():
        parts = over_centers(
            1, residual_halves(), lambda q: dots(residual, residual if q == RR_PART else target)
        )
        held = [next(parts) for _ in range(RD_PART + 1)]
        rr.append(row_to_column(held[RR_PART][:, part_n:]))
        rd.append(row_to_column(held[RD_PART][:, part_n:]))
        beta = rr[1] / rr[0]
        for q in range(PARTS):
            row = held[q] if q <= RD_PART else next(parts)
            n = auctions(q)
            beta_row = jnp.sum(jnp.where(own_slot(n), beta, 0.0), axis=0, keepdims=True)
            yield a_row[:, n] * row[:, :part_n] + beta_row * g_row[:, n]

    sums_two = fold_over_dp(2, second_sums())
    beta = rr[1] / rr[0]
    direction = [residual[h] + beta * target[h] for h in range(2)]
    dd = rr[1] + 2.0 * beta * rd[0] + beta * beta * rr[0]
    for h, (folded, squares) in enumerate(arrived(2, sums_two)):
        if h == 0:
            steps.append(rr[1] / (squares * (1.0 / total_rows) + RIDGE * dd))
        applied = factor_c[h] * folded * (1.0 / total_rows) + RIDGE * direction[h]
        coef_out[:, columns(h)] = steps[0] * target[h] + steps[1] * direction[h]
        resid_out[:, columns(h)] = residual[h] - steps[1] * applied


def hand_out(coef, resid, coef_out, resid_out):
    coef_out[...] = coef[...]
    resid_out[...] = resid[...]


def per_device(total_rows, features, prices, slots, center_idx, center_scale):
    f_dim, rows = features.shape
    cols = center_idx.shape[0]
    half, part_n = cols // 2, rows // PARTS
    exchanges = 2 * 2 + 3 * 2 + 2 * 2 * PARTS
    vmem = pl.BlockSpec(memory_space=pltpu.VMEM)
    both = pl.pallas_call(
        functools.partial(kernel, total_rows),
        out_shape=[jax.ShapeDtypeStruct((SLOTS, cols), F32)] * 2,
        in_specs=[pl.BlockSpec(memory_space=pl.ANY)] * 5,
        out_specs=[vmem] * 2,
        scratch_shapes=[
            pltpu.VMEM((f_dim, rows), BF),
            pltpu.VMEM((1, rows), F32),
            pltpu.VMEM((1, rows), jnp.int32),
            pltpu.VMEM((1, cols), jnp.int32),
            pltpu.VMEM((1, cols), F32),
            pltpu.VMEM((rows, f_dim), BF),
            pltpu.VMEM((rows, cols), BF),
            pltpu.VMEM((rows, cols), BF),
            pltpu.VMEM((cols, rows), BF),
            pltpu.VMEM((cols, rows), BF),
            pltpu.VMEM((1, rows), F32),
            pltpu.VMEM((1, rows), F32),
            pltpu.VMEM((4 * SLOTS, rows), BF),
            pltpu.VMEM((SLOTS, rows), F32),
            pltpu.VMEM((2, CHIPS_X, f_dim, half), BF),
            pltpu.VMEM((2, 2, f_dim, half), BF),
            pltpu.VMEM((3, RING, SLOTS, half + LANE), F32),
            pltpu.VMEM((3, RING, SLOTS, half), F32),
            pltpu.VMEM((2, PARTS, RING, 1, part_n + LANE), F32),
            pltpu.VMEM((2, PARTS, RING, 1, part_n + LANE), F32),
            pltpu.SemaphoreType.DMA((5,)),
            pltpu.SemaphoreType.DMA((exchanges,)),
            pltpu.SemaphoreType.DMA((exchanges,)),
        ],
        compiler_params=pltpu.CompilerParams(
            collective_id=0, has_side_effects=True, vmem_limit_bytes=60 << 20
        ),
        name="cg_steps",
    )(
        features,
        prices.reshape(1, rows),
        slots.reshape(1, rows),
        center_idx.reshape(1, cols),
        center_scale.reshape(1, cols),
    )
    return pl.pallas_call(
        hand_out,
        out_shape=[jax.ShapeDtypeStruct((SLOTS, cols), F32)] * 2,
        in_specs=[vmem] * 2,
        out_specs=[vmem] * 2,
        name="hand_out",
    )(*both)


def solution(mesh):
    def run(features, prices, slots, center_idx, center_scale):
        body = functools.partial(per_device, features.shape[1])
        return jax.shard_map(
            body,
            mesh=mesh,
            in_specs=(P(None, "dp"), P("dp"), P("dp"), P("centers"), P("centers")),
            out_specs=(P(None, "centers"), P(None, "centers")),
            check_vma=False,
        )(features, prices, slots, center_idx, center_scale)

    return run
```

```python
import functools
import math

import jax
import jax.numpy as jnp
from jax import lax
from jax.experimental import pallas as pl
from jax.experimental.pallas import tpu as pltpu
from jax.sharding import PartitionSpec as P

SLOTS = 8
RIDGE = 0.5
MESH = pl.DeviceIdType.MESH
BF = jnp.bfloat16
F32 = jnp.float32

RING = 8
CHIPS_X = 4
FAR_FIRST = (4, 3, 5, 2, 6, 1, 7)
PARTS = 8
RR_PART, RD_PART = 1, 2
LANE = 128


def dot_nn(a, b):
    return lax.dot_general(a, b, (((1,), (0,)), ((), ())), preferred_element_type=F32)


def dot_nt(a, b):
    return lax.dot_general(a, b, (((1,), (1,)), ((), ())), preferred_element_type=F32)


def split_rows(value):
    high = value.astype(BF).astype(F32)
    rest = value - high
    middle = rest.astype(BF).astype(F32)
    return jnp.concatenate([high, middle, rest - middle], axis=0).astype(BF)


def split_sum(rows24):
    return rows24[:SLOTS] + (rows24[SLOTS : 2 * SLOTS] + rows24[2 * SLOTS : 3 * SLOTS])


def column_to_row(column):
    lane = lax.broadcasted_iota(jnp.int32, (SLOTS, LANE), 1)
    sub = lax.broadcasted_iota(jnp.int32, (SLOTS, LANE), 0)
    return jnp.sum(jnp.where(lane == sub, column, 0.0), axis=0, keepdims=True)


def row_to_column(row):
    lane = lax.broadcasted_iota(jnp.int32, (SLOTS, LANE), 1)
    sub = lax.broadcasted_iota(jnp.int32, (SLOTS, LANE), 0)
    return jnp.sum(jnp.where(lane == sub, row, 0.0), axis=1, keepdims=True)


def lane_blocks(value):
    return sum(value[:, j : j + LANE] for j in range(0, value.shape[1], LANE))


def kernel(
    total_rows,
    feat_in, price_in, slots_in, idx_in, scale_in,
    coef_out, resid_out,
    feat, price, slots, idx, scale,
    feat_t, e_hi, e_lo, t_hi, t_lo, a_row, g_row, weights, first_half,
    buf_ax, buf_ac, buf_y0, buf_y1, buf_p1, buf_p2,
    load_sem, send_sem, recv_sem,
):
    f_dim, rows = feat.shape
    cols = idx.shape[1]
    half = cols // 2
    part_n = rows // PARTS
    tile = 256

    dp = lax.axis_index("dp")
    cen = lax.axis_index("centers")
    z_me, y_me = cen // RING, lax.rem(cen, RING)
    x_me, core_me = dp // 2, lax.rem(dp, 2)
    x_at = [lax.rem(x_me + k, CHIPS_X) * 2 for k in range(CHIPS_X)]
    dp_peers = [(x_at[k] + 1 - core_me, cen) for k in (2, 1, 3)]
    dp_peers[1:1] = [(x_at[2] + core_me, cen)]
    dp_peers += [(x_at[1] + core_me, cen), (x_at[3] + core_me, cen), (dp + 1 - 2 * core_me, cen)]
    x_peers = [(x_at[k] + core_me, cen) for k in (2, 1, 3)]
    mate = [(dp + 1 - 2 * core_me, cen)]
    y_peers = [(dp, z_me * RING + lax.rem(y_me + k, RING)) for k in FAR_FIRST]
    z_peers = [(dp, lax.rem(z_me + k, RING) * RING + y_me) for k in FAR_FIRST]

    barrier = pltpu.get_barrier_semaphore()
    everyone = dp_peers + y_peers + z_peers
    loads = [
        pltpu.make_async_copy(src, dst, load_sem.at[j])
        for j, (src, dst) in enumerate(
            ((idx_in, idx), (feat_in, feat), (slots_in, slots), (price_in, price), (scale_in, scale))
        )
    ]
    for load in loads:
        load.start()
    for peer in everyone:
        pl.semaphore_signal(barrier, inc=1, device_id=peer, device_id_type=MESH)

    used = [0]

    def start(buf, me, peers):
        j = used[0]
        used[0] += 1
        for peer in peers:
            pltpu.make_async_remote_copy(
                src_ref=buf.at[me], dst_ref=buf.at[me], send_sem=send_sem.at[j], recv_sem=recv_sem.at[j],
                device_id=peer, device_id_type=MESH,
            ).start()
        return buf.at[pl.ds(0, len(peers))], j

    def finish(handle):
        slots_of_peers, j = handle
        pltpu.make_async_copy(slots_of_peers, slots_of_peers, send_sem.at[j]).wait()
        pltpu.make_async_copy(slots_of_peers, slots_of_peers, recv_sem.at[j]).wait()

    def total(buf, count=RING):
        v = [buf[k] for k in range(count)]
        while len(v) > 1:
            v = [v[k] + v[k + 1] for k in range(0, len(v), 2)]
        return v[0]

    loads[0].wait()
    loads[1].wait()
    local_idx = idx[...] - dp * rows
    for h in range(2):
        picked = jnp.zeros((f_dim, half), F32)
        for t in range(0, rows, tile):
            row = lax.broadcasted_iota(jnp.int32, (tile, half), 0) + t
            hot = jnp.where(row == local_idx[:, h * half : (h + 1) * half], 1.0, 0.0)
            picked = picked + dot_nn(feat[:, t : t + tile], hot.astype(BF))
        buf_ax[h, x_me] = picked.astype(BF)
    for load in loads[2:]:
        load.wait()
    pl.semaphore_wait(barrier, len(everyone))

    sent = [start(buf_ax.at[h], x_me, x_peers) for h in range(2)]
    for t in range(0, rows, tile):
        feat_t[t : t + tile, :] = feat[:, t : t + tile].T
    norm = jnp.zeros((1, rows), F32)
    for t in range(0, f_dim, 16):
        piece = feat[t : t + 16, :].astype(F32)
        norm = norm + jnp.sum(piece * piece, axis=0, keepdims=True)
    a_row[...] = jnp.exp(norm * (-1.0 / (2.0 * f_dim)))

    def own_slot(n):
        span = slots[:, n]
        return span == lax.broadcasted_iota(jnp.int32, (SLOTS, span.shape[1]), 0)

    def columns(h):
        return slice(h * half, (h + 1) * half)

    def auctions(q):
        return slice(q * part_n, (q + 1) * part_n)

    for q in range(PARTS):
        n = auctions(q)
        v24 = split_rows(jnp.where(own_slot(n), a_row[:, n] * price[:, n], 0.0))
        weights[:, n] = jnp.concatenate([v24.astype(F32), jnp.zeros((SLOTS, part_n), F32)], axis=0).astype(BF)

    def fold(v24, n, h):
        m = columns(h)
        return dot_nn(v24, e_hi[n, m]) + dot_nn(v24, e_lo[n, m])

    factor = math.log2(math.e) / f_dim
    centers, center_norm, sums = [], [], []
    for h in range(2):
        finish(sent[h])
        buf_ac[h, core_me] = total(buf_ax.at[h], CHIPS_X)
        sent[h] = start(buf_ac.at[h], core_me, mate)
    for h in range(2):
        finish(sent[h])
        part = total(buf_ac.at[h], 2)
        part32 = part.astype(F32)
        centers.append(part)
        center_norm.append(jnp.sum(part32 * part32, axis=0, keepdims=True))
        for t in range(0, rows, tile):
            value = jnp.exp2(dot_nn(feat_t[t : t + tile, :], part) * factor)
            high = value.astype(BF)
            e_hi[t : t + tile, columns(h)] = high
            e_lo[t : t + tile, columns(h)] = (value - high.astype(F32)).astype(BF)
        buf = (buf_y0 if h == 0 else buf_y1).at[0]
        buf[dp, :, :half] = split_sum(fold(weights[...], slice(0, rows), h))
        if h == 0:
            buf[dp, :, half:] = jnp.zeros((SLOTS, LANE), F32)
        sums.append(start(buf, dp, dp_peers))

    for h in range(2):
        turned = centers[h].T
        for t in range(0, rows, tile):
            value = jnp.exp2(dot_nn(turned, feat[:, t : t + tile]) * factor)
            high = value.astype(BF)
            t_hi[columns(h), t : t + tile] = high
            t_lo[columns(h), t : t + tile] = (value - high.astype(F32)).astype(BF)
    factor_c = [
        scale[:, columns(h)] * jnp.exp(center_norm[h] * (-1.0 / (2.0 * f_dim))) for h in range(2)
    ]

    def apply_half(w, n, h):
        m = columns(h)
        return split_sum(dot_nn(w, t_hi[m, n]) + dot_nn(w, t_lo[m, n]))

    def over_centers(i, halves, column_of):
        w24 = split_rows(factor_c[0] * next(halves))
        for q in range(PARTS):
            n = auctions(q)
            first_half[:, n] = apply_half(w24, n, 0)
        w24 = split_rows(factor_c[1] * next(halves))
        rings = [(y_me, y_peers), (z_me, z_peers)]

        def of_part(buf, q):
            width = part_n + LANE if q in (RR_PART, RD_PART) else part_n
            return buf.at[i, q, :, :, pl.ds(0, width)]

        first = []
        for q in range(PARTS):
            n = auctions(q)
            part = first_half[:, n] + apply_half(w24, n, 1)
            place, peers = rings[q % 2]
            buf = of_part(buf_p1, q)
            chosen = jnp.sum(jnp.where(own_slot(n), part, 0.0), axis=0, keepdims=True)
            if q in (RR_PART, RD_PART):
                chosen = jnp.concatenate([chosen, column_to_row(column_of(q))], axis=1)
            buf[place] = chosen
            first.append(start(buf, place, peers))
        second = []
        for q in range(PARTS):
            finish(first[q])
            place, peers = rings[1 - q % 2]
            buf = of_part(buf_p2, q)
            buf[place] = total(of_part(buf_p1, q))
            second.append(start(buf, place, peers))
        for q in range(PARTS):
            finish(second[q])
            yield total(of_part(buf_p2, q))

    def fold_over_dp(i, parts_of_g):
        acc = [jnp.zeros((3 * SLOTS, half), F32) for _ in range(2)]
        squares = jnp.zeros((SLOTS, LANE), F32)
        sums = []
        for q, row in enumerate(parts_of_g):
            n = auctions(q)
            mask = own_slot(n)
            squares = squares + lane_blocks(jnp.where(mask, row * row, 0.0))
            v24 = split_rows(jnp.where(mask, a_row[:, n] * row, 0.0))
            for h in range(2):
                acc[h] = acc[h] + fold(v24, n, h)
                if q == PARTS - 1:
                    buf = (buf_y0 if h == 0 else buf_y1).at[i]
                    buf[dp, :, :half] = split_sum(acc[h])
                    if h == 0:
                        buf[dp, :, half:] = squares
                    sums.append(start(buf, dp, dp_peers))
        return sums

    def arrived(i, sums):
        finish(sums[0])
        both = total(buf_y0.at[i])
        yield both[:, :half], jnp.sum(both[:, half:], axis=1, keepdims=True)
        finish(sums[1])
        yield total(buf_y1.at[i]), None

    def dots(u, v):
        return sum(jnp.sum(u[h] * v[h], axis=1, keepdims=True) for h in range(2))

    target = []

    def target_halves():
        for h, (folded, _) in enumerate(arrived(0, sums)):
            target.append(factor_c[h] * folded * (1.0 / math.sqrt(total_rows)))
            yield target[h]

    rr = []

    def first_sums():
        parts = over_centers(0, target_halves(), lambda q: dots(target, target))
        for q, row in enumerate(parts):
            if q == RR_PART:
                rr.append(row_to_column(row[:, part_n:]))
            row = a_row[:, auctions(q)] * row[:, :part_n]
            g_row[:, auctions(q)] = row
            yield row

    sums_one = fold_over_dp(1, first_sums())

    residual, steps = [], []

    def residual_halves():
        for h, (folded, squares) in enumerate(arrived(1, sums_one)):
            if h == 0:
                steps.append(rr[0] / (squares * (1.0 / total_rows) + RIDGE * rr[0]))
            applied = factor_c[h] * folded * (1.0 / total_rows) + RIDGE * target[h]
            residual.append(target[h] - steps[0] * applied)
            yield residual[h]

    rd = []

    def second_sums():
        parts = over_centers(
            1, residual_halves(), lambda q: dots(residual, residual if q == RR_PART else target)
        )
        held = [next(parts) for _ in range(RD_PART + 1)]
        rr.append(row_to_column(held[RR_PART][:, part_n:]))
        rd.append(row_to_column(held[RD_PART][:, part_n:]))
        beta = rr[1] / rr[0]
        for q in range(PARTS):
            row = held[q] if q <= RD_PART else next(parts)
            n = auctions(q)
            beta_row = jnp.sum(jnp.where(own_slot(n), beta, 0.0), axis=0, keepdims=True)
            yield a_row[:, n] * row[:, :part_n] + beta_row * g_row[:, n]

    sums_two = fold_over_dp(2, second_sums())
    beta = rr[1] / rr[0]
    direction = [residual[h] + beta * target[h] for h in range(2)]
    dd = rr[1] + 2.0 * beta * rd[0] + beta * beta * rr[0]
    for h, (folded, squares) in enumerate(arrived(2, sums_two)):
        if h == 0:
            steps.append(rr[1] / (squares * (1.0 / total_rows) + RIDGE * dd))
        applied = factor_c[h] * folded * (1.0 / total_rows) + RIDGE * direction[h]
        coef_out[:, columns(h)] = steps[0] * target[h] + steps[1] * direction[h]
        resid_out[:, columns(h)] = residual[h] - steps[1] * applied


def hand_out(coef, resid, coef_out, resid_out):
    coef_out[...] = coef[...]
    resid_out[...] = resid[...]


def per_device(total_rows, features, prices, slots, center_idx, center_scale):
    f_dim, rows = features.shape
    cols = center_idx.shape[0]
    half, part_n = cols // 2, rows // PARTS
    exchanges = 2 * 2 + 3 * 2 + 2 * 2 * PARTS
    vmem = pl.BlockSpec(memory_space=pltpu.VMEM)
    both = pl.pallas_call(
        functools.partial(kernel, total_rows),
        out_shape=[jax.ShapeDtypeStruct((SLOTS, cols), F32)] * 2,
        in_specs=[pl.BlockSpec(memory_space=pl.ANY)] * 5,
        out_specs=[vmem] * 2,
        scratch_shapes=[
            pltpu.VMEM((f_dim, rows), BF),
            pltpu.VMEM((1, rows), F32),
            pltpu.VMEM((1, rows), jnp.int32),
            pltpu.VMEM((1, cols), jnp.int32),
            pltpu.VMEM((1, cols), F32),
            pltpu.VMEM((rows, f_dim), BF),
            pltpu.VMEM((rows, cols), BF),
            pltpu.VMEM((rows, cols), BF),
            pltpu.VMEM((cols, rows), BF),
            pltpu.VMEM((cols, rows), BF),
            pltpu.VMEM((1, rows), F32),
            pltpu.VMEM((1, rows), F32),
            pltpu.VMEM((4 * SLOTS, rows), BF),
            pltpu.VMEM((SLOTS, rows), F32),
            pltpu.VMEM((2, CHIPS_X, f_dim, half), BF),
            pltpu.VMEM((2, 2, f_dim, half), BF),
            pltpu.VMEM((3, RING, SLOTS, half + LANE), F32),
            pltpu.VMEM((3, RING, SLOTS, half), F32),
            pltpu.VMEM((2, PARTS, RING, 1, part_n + LANE), F32),
            pltpu.VMEM((2, PARTS, RING, 1, part_n + LANE), F32),
            pltpu.SemaphoreType.DMA((5,)),
            pltpu.SemaphoreType.DMA((exchanges,)),
            pltpu.SemaphoreType.DMA((exchanges,)),
        ],
        compiler_params=pltpu.CompilerParams(
            collective_id=0, has_side_effects=True, vmem_limit_bytes=48 << 20
        ),
        name="cg_steps",
    )(
        *(
            pltpu.with_memory_space_constraint(array, pltpu.HBM)
            for array in (
                features,
                prices.reshape(1, rows),
                slots.reshape(1, rows),
                center_idx.reshape(1, cols),
                center_scale.reshape(1, cols),
            )
        )
    )
    return pl.pallas_call(
        hand_out,
        out_shape=[jax.ShapeDtypeStruct((SLOTS, cols), F32)] * 2,
        in_specs=[vmem] * 2,
        out_specs=[vmem] * 2,
        compiler_params=pltpu.CompilerParams(vmem_limit_bytes=4 << 20),
        name="hand_out",
    )(*both)


def solution(mesh):
    def run(features, prices, slots, center_idx, center_scale):
        body = functools.partial(per_device, features.shape[1])
        return jax.shard_map(
            body,
            mesh=mesh,
            in_specs=(P(None, "dp"), P("dp"), P("dp"), P("centers"), P("centers")),
            out_specs=(P(None, "centers"), P(None, "centers")),
            check_vma=False,
        )(features, prices, slots, center_idx, center_scale)

    return run
```

```python
import functools
import math

import jax
import jax.numpy as jnp
from jax import lax
from jax.experimental import pallas as pl
from jax.experimental.pallas import tpu as pltpu
from jax.sharding import PartitionSpec as P

SLOTS = 8
RIDGE = 0.5
MESH = pl.DeviceIdType.MESH
BF = jnp.bfloat16
F32 = jnp.float32

RING = 8
CHIPS_X = 4
FAR_FIRST = (4, 3, 5, 2, 6, 1, 7)
APPLY_PARTS, PARTS = 8, 8
RR_IN, RD_IN = 1, 2
RR_PART, RD_PART = RR_IN * PARTS // APPLY_PARTS, RD_IN * PARTS // APPLY_PARTS
LANE = 128


def dot_nn(a, b):
    return lax.dot_general(a, b, (((1,), (0,)), ((), ())), preferred_element_type=F32)


def dot_nt(a, b):
    return lax.dot_general(a, b, (((1,), (1,)), ((), ())), preferred_element_type=F32)


def split_rows(value):
    high = value.astype(BF).astype(F32)
    rest = value - high
    middle = rest.astype(BF).astype(F32)
    return jnp.concatenate([high, middle, rest - middle], axis=0).astype(BF)


def split_sum(rows24):
    return rows24[:SLOTS] + (rows24[SLOTS : 2 * SLOTS] + rows24[2 * SLOTS : 3 * SLOTS])


def column_to_row(column):
    lane = lax.broadcasted_iota(jnp.int32, (SLOTS, LANE), 1)
    sub = lax.broadcasted_iota(jnp.int32, (SLOTS, LANE), 0)
    return jnp.sum(jnp.where(lane == sub, column, 0.0), axis=0, keepdims=True)


def row_to_column(row):
    lane = lax.broadcasted_iota(jnp.int32, (SLOTS, LANE), 1)
    sub = lax.broadcasted_iota(jnp.int32, (SLOTS, LANE), 0)
    return jnp.sum(jnp.where(lane == sub, row, 0.0), axis=1, keepdims=True)


def lane_blocks(value):
    return sum(value[:, j : j + LANE] for j in range(0, value.shape[1], LANE))


def kernel(
    total_rows,
    feat_in, price_in, slots_in, idx_in, scale_in,
    coef_out, resid_out,
    feat, price, slots, idx, scale,
    feat_t, e_hi, e_lo, t_hi, t_lo, a_row, g_row, weights,
    buf_ax, buf_ac, buf_y0, buf_y1, buf_p1, buf_p2,
    load_sem, send_sem, recv_sem,
):
    f_dim, rows = feat.shape
    cols = idx.shape[1]
    half = cols // 2
    part_n = rows // PARTS
    apply_n = rows // APPLY_PARTS
    tile = 256

    dp = lax.axis_index("dp")
    cen = lax.axis_index("centers")
    z_me, y_me = cen // RING, lax.rem(cen, RING)
    x_me, core_me = dp // 2, lax.rem(dp, 2)
    x_at = [lax.rem(x_me + k, CHIPS_X) * 2 for k in range(CHIPS_X)]
    dp_peers = [(x_at[k] + 1 - core_me, cen) for k in (2, 1, 3)]
    dp_peers[1:1] = [(x_at[2] + core_me, cen)]
    dp_peers += [(x_at[1] + core_me, cen), (x_at[3] + core_me, cen), (dp + 1 - 2 * core_me, cen)]
    x_peers = [(x_at[k] + core_me, cen) for k in (2, 1, 3)]
    mate = [(dp + 1 - 2 * core_me, cen)]
    y_peers = [(dp, z_me * RING + lax.rem(y_me + k, RING)) for k in FAR_FIRST]
    z_peers = [(dp, lax.rem(z_me + k, RING) * RING + y_me) for k in FAR_FIRST]

    barrier = pltpu.get_barrier_semaphore()
    everyone = y_peers + z_peers + dp_peers
    for peer in everyone:
        pl.semaphore_signal(barrier, inc=1, device_id=peer, device_id_type=MESH)
    loads = [
        pltpu.make_async_copy(src, dst, load_sem.at[j])
        for j, (src, dst) in enumerate(
            ((idx_in, idx), (feat_in, feat), (slots_in, slots), (price_in, price), (scale_in, scale))
        )
    ]
    for load in loads:
        load.start()

    used = [0]

    def start(buf, me, peers):
        j = used[0]
        used[0] += 1
        for peer in peers:
            pltpu.make_async_remote_copy(
                src_ref=buf.at[me], dst_ref=buf.at[me], send_sem=send_sem.at[j], recv_sem=recv_sem.at[j],
                device_id=peer, device_id_type=MESH,
            ).start()
        return buf.at[pl.ds(0, len(peers))], j

    def finish(handle):
        slots_of_peers, j = handle
        pltpu.make_async_copy(slots_of_peers, slots_of_peers, send_sem.at[j]).wait()
        pltpu.make_async_copy(slots_of_peers, slots_of_peers, recv_sem.at[j]).wait()

    def total(buf, count=RING):
        v = [buf[k] for k in range(count)]
        while len(v) > 1:
            v = [v[k] + v[k + 1] for k in range(0, len(v), 2)]
        return v[0]

    loads[0].wait()
    loads[1].wait()
    local_idx = idx[...] - dp * rows
    for h in range(2):
        picked = jnp.zeros((f_dim, half), F32)
        for t in range(0, rows, tile):
            row = lax.broadcasted_iota(jnp.int32, (tile, half), 0) + t
            hot = jnp.where(row == local_idx[:, h * half : (h + 1) * half], 1.0, 0.0)
            picked = picked + dot_nn(feat[:, t : t + tile], hot.astype(BF))
        buf_ax[h, x_me] = picked.astype(BF)
    for load in loads[2:]:
        load.wait()
    pl.semaphore_wait(barrier, len(everyone))

    sent = [start(buf_ax.at[h], x_me, x_peers) for h in range(2)]
    for t in range(0, rows, tile):
        feat_t[t : t + tile, :] = feat[:, t : t + tile].T
    norm = jnp.zeros((1, rows), F32)
    for t in range(0, f_dim, 16):
        piece = feat[t : t + 16, :].astype(F32)
        norm = norm + jnp.sum(piece * piece, axis=0, keepdims=True)
    a_row[...] = jnp.exp(norm * (-1.0 / (2.0 * f_dim)))

    def own_slot(n):
        span = slots[:, n]
        return span == lax.broadcasted_iota(jnp.int32, (SLOTS, span.shape[1]), 0)

    def columns(h):
        return slice(h * half, (h + 1) * half)

    def auctions(q):
        return slice(q * part_n, (q + 1) * part_n)

    for q in range(PARTS):
        n = auctions(q)
        v24 = split_rows(jnp.where(own_slot(n), a_row[:, n] * price[:, n], 0.0))
        weights[:, n] = jnp.concatenate([v24.astype(F32), jnp.zeros((SLOTS, part_n), F32)], axis=0).astype(BF)

    def fold(v24, n, m):
        return dot_nn(v24, e_hi[n, m]) + dot_nn(v24, e_lo[n, m])

    factor = math.log2(math.e) / f_dim
    centers, center_norm, sums = [], [], []
    for h in range(2):
        finish(sent[h])
        buf_ac[h, core_me] = total(buf_ax.at[h], CHIPS_X)
        sent[h] = start(buf_ac.at[h], core_me, mate)
    for h in range(2):
        finish(sent[h])
        part = total(buf_ac.at[h], 2)
        part32 = part.astype(F32)
        centers.append(part)
        center_norm.append(jnp.sum(part32 * part32, axis=0, keepdims=True))
        acc = jnp.zeros((weights.shape[0], half), F32)
        for t in range(0, rows, tile):
            value = jnp.exp2(dot_nn(feat_t[t : t + tile, :], part) * factor)
            high = value.astype(BF)
            low = (value - high.astype(F32)).astype(BF)
            e_hi[t : t + tile, columns(h)] = high
            e_lo[t : t + tile, columns(h)] = low
            piece = weights[:, t : t + tile]
            acc = acc + (dot_nn(piece, high) + dot_nn(piece, low))
        buf = (buf_y0 if h == 0 else buf_y1).at[0]
        buf[dp, :, :half] = split_sum(acc)
        if h == 0:
            buf[dp, :, half:] = jnp.zeros((SLOTS, LANE), F32)
        sums.append(start(buf, dp, dp_peers))

    for h in range(2):
        turned = centers[h].T
        for t in range(0, rows, tile):
            value = jnp.exp2(dot_nn(turned, feat[:, t : t + tile]) * factor)
            high = value.astype(BF)
            t_hi[columns(h), t : t + tile] = high
            t_lo[columns(h), t : t + tile] = (value - high.astype(F32)).astype(BF)
    factor_c = [
        scale[:, columns(h)] * jnp.exp(center_norm[h] * (-1.0 / (2.0 * f_dim))) for h in range(2)
    ]

    def over_centers(i, halves, column_of):
        w24 = split_rows(jnp.concatenate([factor_c[h] * next(halves) for h in range(2)], axis=1))
        rings = [(y_me, y_peers), (z_me, z_peers)]
        few = min(APPLY_PARTS, PARTS)
        joined, cut = APPLY_PARTS // few, PARTS // few

        def sent_part(q):
            return buf_p1.at[i, q, :, :, pl.ds(0, apply_n + (LANE if q in (RR_IN, RD_IN) else 0))]

        def summed_part(q):
            return buf_p2.at[i, q, :, :, pl.ds(0, part_n + (LANE if q in (RR_PART, RD_PART) else 0))]

        def products(q):
            n = slice(q * apply_n, (q + 1) * apply_n)
            return split_sum(dot_nn(w24, t_hi[:, n]) + dot_nn(w24, t_lo[:, n]))

        first = []
        ahead = products(0)
        for q in range(APPLY_PARTS):
            n = slice(q * apply_n, (q + 1) * apply_n)
            part = ahead
            if q + 1 < APPLY_PARTS:
                ahead = products(q + 1)
            place, peers = rings[q // joined % 2]
            buf = sent_part(q)
            chosen = jnp.sum(jnp.where(own_slot(n), part, 0.0), axis=0, keepdims=True)
            if q in (RR_IN, RD_IN):
                chosen = jnp.concatenate([chosen, column_to_row(column_of(q))], axis=1)
            buf[place] = chosen
            first.append(start(buf, place, peers))
        second = []
        for p in range(few):
            pieces, extras = [], []
            for q in range(p * joined, (p + 1) * joined):
                finish(first[q])
                row = total(sent_part(q))
                pieces.append(row[:, :apply_n])
                if q in (RR_IN, RD_IN):
                    extras.append(row[:, apply_n:])
            row = jnp.concatenate(pieces, axis=1) if joined > 1 else pieces[0]
            place, peers = rings[1 - p % 2]
            for k in range(cut):
                q = p * cut + k
                piece = row[:, k * part_n : (k + 1) * part_n]
                if q in (RR_PART, RD_PART):
                    piece = jnp.concatenate([piece, extras.pop(0)], axis=1)
                buf = summed_part(q)
                buf[place] = piece
                second.append(start(buf, place, peers))
        for q in range(PARTS):
            finish(second[q])
            yield total(summed_part(q))

    def fold_over_dp(i, parts_of_g):
        acc = jnp.zeros((3 * SLOTS, cols), F32)
        squares = jnp.zeros((SLOTS, LANE), F32)
        sums = []
        for q, row in enumerate(parts_of_g):
            n = auctions(q)
            mask = own_slot(n)
            squares = squares + lane_blocks(jnp.where(mask, row * row, 0.0))
            v24 = split_rows(jnp.where(mask, a_row[:, n] * row, 0.0))
            if q < PARTS - 1:
                acc = acc + fold(v24, n, slice(0, cols))
                continue
            for h in range(2):
                buf = (buf_y0 if h == 0 else buf_y1).at[i]
                buf[dp, :, :half] = split_sum(acc[:, columns(h)] + fold(v24, n, columns(h)))
                if h == 0:
                    buf[dp, :, half:] = squares
                sums.append(start(buf, dp, dp_peers))
        return sums

    def arrived(i, sums):
        finish(sums[0])
        both = total(buf_y0.at[i])
        yield both[:, :half], jnp.sum(both[:, half:], axis=1, keepdims=True)
        finish(sums[1])
        yield total(buf_y1.at[i]), None

    def dots(u, v):
        return sum(jnp.sum(u[h] * v[h], axis=1, keepdims=True) for h in range(2))

    target = []

    def target_halves():
        for h, (folded, _) in enumerate(arrived(0, sums)):
            target.append(factor_c[h] * folded * (1.0 / math.sqrt(total_rows)))
            yield target[h]

    rr = []

    def first_sums():
        parts = over_centers(0, target_halves(), lambda q: dots(target, target))
        for q, row in enumerate(parts):
            if q == RR_PART:
                rr.append(row_to_column(row[:, part_n:]))
            row = a_row[:, auctions(q)] * row[:, :part_n]
            g_row[:, auctions(q)] = row
            yield row

    sums_one = fold_over_dp(1, first_sums())

    residual, steps = [], []

    def residual_halves():
        for h, (folded, squares) in enumerate(arrived(1, sums_one)):
            if h == 0:
                steps.append(rr[0] / (squares * (1.0 / total_rows) + RIDGE * rr[0]))
            applied = factor_c[h] * folded * (1.0 / total_rows) + RIDGE * target[h]
            residual.append(target[h] - steps[0] * applied)
            yield residual[h]

    rd = []

    def second_sums():
        parts = over_centers(
            1, residual_halves(), lambda q: dots(residual, residual if q == RR_IN else target)
        )
        held = [next(parts) for _ in range(RD_PART + 1)]
        rr.append(row_to_column(held[RR_PART][:, part_n:]))
        rd.append(row_to_column(held[RD_PART][:, part_n:]))
        beta = rr[1] / rr[0]
        for q in range(PARTS):
            row = held[q] if q <= RD_PART else next(parts)
            n = auctions(q)
            beta_row = jnp.sum(jnp.where(own_slot(n), beta, 0.0), axis=0, keepdims=True)
            yield a_row[:, n] * row[:, :part_n] + beta_row * g_row[:, n]

    sums_two = fold_over_dp(2, second_sums())
    beta = rr[1] / rr[0]
    direction = [residual[h] + beta * target[h] for h in range(2)]
    dd = rr[1] + 2.0 * beta * rd[0] + beta * beta * rr[0]
    for h, (folded, squares) in enumerate(arrived(2, sums_two)):
        if h == 0:
            steps.append(rr[1] / (squares * (1.0 / total_rows) + RIDGE * dd))
        applied = factor_c[h] * folded * (1.0 / total_rows) + RIDGE * direction[h]
        coef_out[:, columns(h)] = steps[0] * target[h] + steps[1] * direction[h]
        resid_out[:, columns(h)] = residual[h] - steps[1] * applied


def hand_out(coef, resid, coef_out, resid_out):
    coef_out[...] = coef[...]
    resid_out[...] = resid[...]


def per_device(total_rows, features, prices, slots, center_idx, center_scale):
    f_dim, rows = features.shape
    cols = center_idx.shape[0]
    half, part_n, apply_n = cols // 2, rows // PARTS, rows // APPLY_PARTS
    exchanges = 2 * 2 + 3 * 2 + 2 * (APPLY_PARTS + PARTS)
    vmem = pl.BlockSpec(memory_space=pltpu.VMEM)
    both = pl.pallas_call(
        functools.partial(kernel, total_rows),
        out_shape=[jax.ShapeDtypeStruct((SLOTS, cols), F32)] * 2,
        in_specs=[pl.BlockSpec(memory_space=pl.ANY)] * 5,
        out_specs=[vmem] * 2,
        scratch_shapes=[
            pltpu.VMEM((f_dim, rows), BF),
            pltpu.VMEM((1, rows), F32),
            pltpu.VMEM((1, rows), jnp.int32),
            pltpu.VMEM((1, cols), jnp.int32),
            pltpu.VMEM((1, cols), F32),
            pltpu.VMEM((rows, f_dim), BF),
            pltpu.VMEM((rows, cols), BF),
            pltpu.VMEM((rows, cols), BF),
            pltpu.VMEM((cols, rows), BF),
            pltpu.VMEM((cols, rows), BF),
            pltpu.VMEM((1, rows), F32),
            pltpu.VMEM((1, rows), F32),
            pltpu.VMEM((4 * SLOTS, rows), BF),
            pltpu.VMEM((2, CHIPS_X, f_dim, half), BF),
            pltpu.VMEM((2, 2, f_dim, half), BF),
            pltpu.VMEM((3, RING, SLOTS, half + LANE), F32),
            pltpu.VMEM((3, RING, SLOTS, half), F32),
            pltpu.VMEM((2, APPLY_PARTS, RING, 1, apply_n + LANE), F32),
            pltpu.VMEM((2, PARTS, RING, 1, part_n + LANE), F32),
            pltpu.SemaphoreType.DMA((5,)),
            pltpu.SemaphoreType.DMA((exchanges,)),
            pltpu.SemaphoreType.DMA((exchanges,)),
        ],
        compiler_params=pltpu.CompilerParams(
            collective_id=0, has_side_effects=True, vmem_limit_bytes=48 << 20
        ),
        name="cg_steps",
    )(
        *(
            pltpu.with_memory_space_constraint(array, pltpu.HBM)
            for array in (
                features,
                prices.reshape(1, rows),
                slots.reshape(1, rows),
                center_idx.reshape(1, cols),
                center_scale.reshape(1, cols),
            )
        )
    )
    return pl.pallas_call(
        hand_out,
        out_shape=[jax.ShapeDtypeStruct((SLOTS, cols), F32)] * 2,
        in_specs=[vmem] * 2,
        out_specs=[vmem] * 2,
        compiler_params=pltpu.CompilerParams(vmem_limit_bytes=4 << 20),
        name="hand_out",
    )(*both)


def solution(mesh):
    def run(features, prices, slots, center_idx, center_scale):
        body = functools.partial(per_device, features.shape[1])
        return jax.shard_map(
            body,
            mesh=mesh,
            in_specs=(P(None, "dp"), P("dp"), P("dp"), P("centers"), P("centers")),
            out_specs=(P(None, "centers"), P(None, "centers")),
            check_vma=False,
        )(features, prices, slots, center_idx, center_scale)

    return run
```
